1024 devices in a mesh: expert: 32 (over y, z_lo), dp: 32 (over z_hi, x, core).
Axes of the slice: x: 4, y: 8, z: 16 (z_hi: 4, z_lo: 4; z = z_hi * 4 + z_lo), core: 2. Of those that a mesh axis runs over, the one named last changes fastest.
Arguments:
- tokens: bfloat16 [131072, 2048], P(('expert', 'dp')), may hold values from -24 to 24
- routes: int32 [131072, 1], P(('expert', 'dp')), may hold values from 0 to 31; in each aligned block of 128 rows (0 to 127, 128 to 255, ...) at most 6 rows name the same one
- route_weight: float32 [131072, 1], P(('expert', 'dp')), may hold values from 0.25 to 1
- w_in: bfloat16 [32, 2048, 768], P('expert'), may hold values from -0.125 to 0.125
- w_out: bfloat16 [32, 2048, 384], P('expert'), may hold values from -0.3125 to 0.3125
- out_grad: bfloat16 [131072, 2048], P(('expert', 'dp')), may hold values from -6 to 6
Outputs:
- mixed: bfloat16 [131072, 2048], P(('expert', 'dp'))
- token_grad: bfloat16 [131072, 2048], P(('expert', 'dp'))
- grad_in: bfloat16 [32, 2048, 768], P('expert', 'dp')
- grad_out: bfloat16 [32, 2048, 384], P('expert', 'dp')
The draws below stay inside these ranges and needn't reach their ends.
Inputs may be any that keep to these rules, and one draw needn't show every extreme that they name: `routes`: in the 128 rows of one device no expert is named more than 6 times, and in every draw some device names some expert exactly 6 times.
All inputs are finite; a program needn't handle non-finite values.
Results may differ from the reference program's by a relative error of at most 0.02.
Values may be sent and summed in bfloat16 or wider, within the bound.
A program may use at most 64 MiB of HBM per device.

```python
import math
import jax
import jax.numpy as jnp
import numpy as np
from jax import lax

D = 2048
FW = 384
TOK_DEV = 128
EXPERTS = 32
TOKENS = 131072
CAP = 6
N_EXPERT = 32
N_DP = 32


def strengthened(drawn, key, source, target, blocks, factor):
    def block_of(dim):
        return (jnp.arange(drawn.shape[dim]) // (drawn.shape[dim] // blocks)).reshape((-1,) + (1,) * (drawn.ndim - 1 - dim))

    one_side = jax.random.permutation(key, blocks)[block_of(target)]
    second = (block_of(target) + blocks // 2) % blocks
    return jnp.where((block_of(source) == one_side) | (block_of(source) == second), factor * drawn, drawn)


def level_of(rng, dims, split, smallest, top_value):
    level, own = 1.0, jax.random.fold_in(rng, 6)
    for axis_at, parts in split:
        heights = jnp.exp(jax.random.uniform(jax.random.fold_in(own, axis_at), (parts,), jnp.float32, smallest / len(split), top_value / len(split)))
        level = level * jnp.repeat(heights, dims[axis_at] // parts).reshape([-1 if axis == axis_at else 1 for axis in range(len(dims))])
    return level


def assign_block(stream_key, own, number, rows, number_of, top, most, skew):
    order = jax.random.permutation(stream_key, number_of)
    packed, usual = shares(number_of, rows * top, most, skew, True), shares(number_of, rows * top, most, skew, False)
    places = jnp.arange(number_of)

    def named(sizes, rotation):
        used = int((sizes > 0).sum())
        fixed = max(1, used // 4)
        moved = fixed + (places - fixed + rotation * (used - fixed)) % max(1, number_of - fixed)
        return jnp.zeros((number_of,), jnp.int32).at[order[jnp.where(places < fixed, places, moved)]].set(jnp.asarray(sizes, jnp.int32))

    sizes = jnp.where(number % 4 == 0, named(packed, number // 4), named(usual, number - number // 4 - 1))
    mixed = jax.random.permutation(jax.random.fold_in(own, 3), number_of)
    donor, sink = mixed[0:number_of // 2 * 2:2], mixed[1:number_of // 2 * 2:2]
    margin = jnp.minimum(sizes[donor] - 1, most - sizes[sink]) // 2
    margin = jnp.where((donor == order[0]) | (sink == order[0]) | (sizes[sink] == 0), 0, jnp.maximum(margin, 0))
    moved = jax.random.randint(jax.random.fold_in(own, 4), (number_of // 2,), 0, 1 << 20) % (margin + 1)
    sizes = sizes.at[donor].add(-moved).at[sink].add(moved)
    labels = jnp.searchsorted(jnp.cumsum(sizes), jnp.arange(rows * top), side="right").astype(jnp.int32)
    grid = labels.reshape(top, rows).T
    grid = grid[jax.random.permutation(jax.random.fold_in(own, 1), rows)]
    rotation = jax.random.randint(jax.random.fold_in(own, 2), (rows, 1), 0, top)
    return jnp.take_along_axis(grid, (jnp.arange(top)[None, :] + rotation) % top, axis=1)


def shares(amount, total, reach, skew, full):
    loads = [(1 << 20) // math.isqrt(grade ** skew) + 1 for grade in range(1, amount + 1)]
    largest = reach if full else min(reach, max(-(-total // amount), total * loads[0] // sum(loads)))
    least = 1 if total - largest >= amount - 1 else 0
    counts, surplus = [largest] + [least] * (amount - 1), total - largest - least * (amount - 1)
    while surplus > 0:
        movable = [i for i in range(1, amount) if counts[i] < largest] or [i for i in range(1, amount) if counts[i] < reach]
        mass, left = sum([loads[i] for i in movable]), surplus
        for i in movable:
            more = min(reach - counts[i], max(1, left * loads[i] // mass), surplus)
            counts[i] = counts[i] + more
            surplus = surplus - more
    return np.array(counts)


def scatter_about(rng, shape, scale, bound, cuts=(), held_as=jnp.bfloat16):
    entries = jax.random.normal(rng, shape, jnp.float32) * scale
    if len(cuts) > 0:
        entries = level_of(rng, shape, cuts, -0.22, 0.18) * entries
    return jnp.clip(entries, min=-bound, max=bound).astype(held_as)


def noise_with(stream_key, extent, scale, limit, shards, heavy, kind=jnp.bfloat16):
    result = scale * jax.random.normal(stream_key, extent, jnp.float32)
    if shards:
        result = result * level_of(stream_key, extent, shards, -0.22, 0.18)
    return jnp.clip(strengthened(result, jax.random.fold_in(stream_key, 3), *heavy), -limit, limit).astype(kind)


def setup_inputs(seed: int = 0) -> dict:
    arg_keys = jax.random.split(jax.random.key(seed), 7)
    tokens = noise_with(arg_keys[0], (TOKENS, D), 1.0, 24.0, ((0, 1024),), (0, 1, 1024, 6.0))
    routes_keys = jax.random.split(jax.random.fold_in(arg_keys[1], 1), TOKENS // TOK_DEV)
    routes_turns = jax.random.permutation(jax.random.fold_in(arg_keys[1], 3), TOKENS // TOK_DEV)
    routes = jax.vmap(lambda own, number: assign_block(jax.random.fold_in(arg_keys[1], 2), own, number, TOK_DEV, EXPERTS, 1, CAP, 2))(routes_keys, routes_turns).reshape((TOKENS, 1))
    route_weight = jnp.clip(jnp.exp(math.log(1.0) - 1.3862944 * jax.random.uniform(arg_keys[2], (TOKENS, 1), jnp.float32) ** level_of(arg_keys[2], (TOKENS, 1), ((0, 1024),), -0.2, 0.2)), 0.25, 1.0)
    w_in = scatter_about(arg_keys[3], (EXPERTS, D, 2 * FW), D ** -0.5, 0.125, ((0, 32),))
    w_out = scatter_about(arg_keys[4], (EXPERTS, D, FW), FW ** -0.5, 0.3125, ((0, 32),))
    out_grad = scatter_about(arg_keys[5], (TOKENS, D), 1.0, 6.0, ((0, 1024),))
    return {"tokens": tokens, "routes": routes, "route_weight": route_weight, "w_in": w_in, "w_out": w_out, "out_grad": out_grad}


def rounded(value):
    return lax.optimization_barrier(value.astype(jnp.bfloat16)).astype(jnp.float32)


def placement_matrix(route_block, experts, capacity):
    chosen = route_block[:, 0]
    onehot = (chosen[:, None] == jnp.arange(experts, dtype=jnp.int32)[None, :]).astype(jnp.int32)
    ranks = jnp.sum(jnp.cumsum(onehot, axis=0) * onehot, axis=1) - 1
    target = chosen * capacity + ranks
    slots = jnp.arange(experts * capacity, dtype=jnp.int32)
    return (slots[:, None] == target[None, :]).astype(jnp.float32)


def expert_pass(rows_in, rows_cot, w_first, w_second):
    width = w_second.shape[2]
    gate_up = jnp.einsum("erd,edf->erf", rows_in, w_first)
    gate = gate_up[..., :width]
    upper = gate_up[..., width:]
    sigmoid_gate = jax.nn.sigmoid(gate)
    activated = gate * sigmoid_gate
    hidden = rounded(activated * upper)
    outputs = rounded(jnp.einsum("erf,edf->erd", hidden, w_second))
    grad_hidden = jnp.einsum("erd,edf->erf", rows_cot, w_second)
    grad_gate = grad_hidden * upper * sigmoid_gate * (1.0 + gate * (1.0 - sigmoid_gate))
    grad_upper = grad_hidden * activated
    grad_both = rounded(jnp.concatenate([grad_gate, grad_upper], axis=-1))
    grad_rows = rounded(jnp.einsum("erf,edf->erd", grad_both, w_first))
    term_first = jnp.einsum("erd,erf->edf", rows_in, grad_both)
    term_second = jnp.einsum("erd,erf->edf", rows_cot, hidden)
    return outputs, grad_rows, term_first, term_second


def reference(tokens, routes, route_weight, w_in, w_out, out_grad):
    token_parts = tokens.astype(jnp.float32).reshape(N_EXPERT, N_DP, TOK_DEV, D).transpose(1, 0, 2, 3)
    cotangent = rounded(route_weight * out_grad.astype(jnp.float32))
    cot_parts = cotangent.reshape(N_EXPERT, N_DP, TOK_DEV, D).transpose(1, 0, 2, 3)
    route_parts = routes.reshape(N_EXPERT, N_DP, TOK_DEV, 1).transpose(1, 0, 2, 3)
    w_first = w_in.astype(jnp.float32)
    w_second = w_out.astype(jnp.float32)

    def one_replica(carry, inputs):
        token_block, cot_block, route_block = inputs
        placer = jax.vmap(lambda block: placement_matrix(block, EXPERTS, CAP))(route_block)

        def to_experts(values):
            sent = jnp.einsum("jct,jtd->jcd", placer, values)
            sent = sent.reshape(N_EXPERT, EXPERTS, CAP, D).transpose(1, 0, 2, 3)
            return sent.reshape(EXPERTS, N_EXPERT * CAP, D)

        def to_tokens(values):
            back = values.reshape(EXPERTS, N_EXPERT, CAP, D).transpose(1, 0, 2, 3)
            back = back.reshape(N_EXPERT, EXPERTS * CAP, D)
            return jnp.einsum("jct,jcd->jtd", placer, back)

        outputs, grad_rows, term_first, term_second = expert_pass(
            to_experts(token_block), to_experts(cot_block), w_first, w_second)
        acc_first, acc_second = carry
        acc_first = acc_first + rounded(term_first)
        acc_second = acc_second + rounded(term_second)
        return (acc_first, acc_second), (to_tokens(outputs), to_tokens(grad_rows))

    start = (jnp.zeros((EXPERTS, D, 2 * FW), jnp.float32), jnp.zeros((EXPERTS, D, FW), jnp.float32))
    (acc_first, acc_second), (token_out, token_back) = lax.scan(one_replica, start, (token_parts, cot_parts, route_parts))
    token_out = token_out.transpose(1, 0, 2, 3).reshape(TOKENS, D)
    token_back = token_back.transpose(1, 0, 2, 3).reshape(TOKENS, D)
    mixed = (route_weight * token_out).astype(jnp.bfloat16)
    token_grad = token_back.astype(jnp.bfloat16)
    grad_in = (acc_first / N_DP).astype(jnp.bfloat16)
    grad_out = (acc_second / N_DP).astype(jnp.bfloat16)
    return (mixed, token_grad, grad_in, grad_out)
```

```python
import functools

import jax
import jax.numpy as jnp
from jax import lax
from jax.experimental import pallas as pl
from jax.experimental.pallas import tpu as pltpu
from jax.sharding import PartitionSpec as P

MESH = pl.DeviceIdType.MESH
BF = jnp.bfloat16
F32 = jnp.float32

D = 2048
F1 = 768
F2 = 384
FF = F1 + F2
ROWS = 192
TOK = 128
LANES = 128
TILE = 16
FHALF = FF // 2
FQ = FHALF // 2
FD = FQ // 2
NT = (((1,), (1,)), ((), ()))
WINDOW = (-1, 0, 1, 2)


def slot_tables(routes):
    chosen = routes[:, 0]
    at = jnp.arange(TOK, dtype=jnp.int32)
    earlier = (chosen[:, None] == chosen[None, :]) & (at[None, :] < at[:, None])
    rank = jnp.sum(earlier.astype(jnp.int32), axis=1)
    group = (rank // 3) * 32 + chosen
    inner = rank % 3
    place = group * 3 + inner
    slots = jnp.arange(ROWS, dtype=jnp.int32)
    source = TOK + jnp.sum(
        jnp.where(place[None, :] == slots[:, None], at[None, :] - TOK, 0), axis=1
    )
    return source, group, inner


def kernel(
    source, group, inner, tokens, out_grad, weight, w1_any, w2_any,
    mixed, token_grad, grad_in, grad_out,
    w1, w2, perm, tiles_t, tiles_c, stage, mid, landed, mat_x, mat_c, gates, qh, qht, mat_y,
    ytile, zback, back_y, back_r, part, other, summed,
    xrelay, xacc, from_l, from_r, zsum, zrelay, zacc, zfrom_l, zfrom_r, final,
    w_sem, ys, yr, yl, zs, zr, zl_sem, rzs, rzr, rzl, rys, ryr, ryl,
    cs, cr, xs, xr, gs, gr, fs, fr,
):
    e = lax.axis_index("expert")
    d = lax.axis_index("dp")
    y, zl = e // 4, e % 4
    zh, x, c = d // 8, (d // 2) % 4, d % 2
    z = zh * 4 + zl
    sign = 1 - 2 * c

    def device(y_at, z_at, x_at, c_at):
        return {"expert": y_at * 4 + z_at % 4, "dp": (z_at // 4) * 8 + x_at * 2 + c_at}

    def y_dev(step):
        return device((y + step) % 8, z, x, c)

    def z_dev(step):
        return device(y, (z + step + 16) % 16, x, c)

    def x_dev(step):
        return device(y, z, (x + step + 4) % 4, c)

    twin = device(y, z, x, 1 - c)

    def remote(src, dst, send, recv, to):
        return pltpu.make_async_remote_copy(
            src_ref=src, dst_ref=dst, send_sem=send, recv_sem=recv, device_id=to, device_id_type=MESH
        )

    barrier = pltpu.get_barrier_semaphore()

    def greet(to):
        pl.semaphore_signal(barrier, inc=1, device_id=to, device_id_type=MESH)

    for step in range(1, 8):
        greet(y_dev(step))
    for step in (-4, -2, -1, 1, 2, 4):
        greet(z_dev(step))
    for step in (-1, 1):
        greet(x_dev(step))
    greet(twin)

    w_copies = (
        pltpu.make_async_copy(w1_any.at[0], w1, w_sem.at[0]),
        pltpu.make_async_copy(w2_any.at[0], w2, w_sem.at[1]),
    )
    for copy in w_copies:
        copy.start()

    row_at = lax.broadcasted_iota(jnp.int32, (256, 256), 0)
    col_at = lax.broadcasted_iota(jnp.int32, (256, 256), 1)
    perm[...] = jnp.where(col_at == (row_at % 16) * 16 + row_at // 16, 1.0, 0.0).astype(BF)

    def to_tiles(rows32):
        cols = [
            jnp.concatenate(
                [rows32[:16, k * LANES : (k + 1) * LANES], rows32[16:, k * LANES : (k + 1) * LANES]], axis=1
            )
            for k in range(16)
        ]
        out = jnp.dot(perm[...], jnp.concatenate(cols, axis=0), preferred_element_type=F32).astype(BF)
        return out[:, :LANES].reshape(16, TILE, LANES), out[:, LANES:].reshape(16, TILE, LANES)

    def from_tiles(first, second):
        both = jnp.concatenate([first.reshape(256, LANES), second.reshape(256, LANES)], axis=1)
        return jnp.dot(perm[...], both, preferred_element_type=F32)

    tiles_t[TOK] = jnp.zeros((TILE, LANES), BF)
    tiles_c[TOK] = jnp.zeros((TILE, LANES), BF)

    def y_copy(a, h, step):
        there = (y + step) % 8
        return remote(
            stage.at[a, h, pl.ds(there * 4, 4)],
            mid.at[a, h, :, pl.ds(y * 3, 3)],
            ys.at[a, h, step - 1],
            yr.at[a, h, step - 1],
            y_dev(step),
        )

    def y_self(a, h):
        return pltpu.make_async_copy(
            stage.at[a, h, pl.ds(y * 4, 4)], mid.at[a, h, :, pl.ds(y * 3, 3)], yl.at[a, h]
        )

    def step_of(n):
        half = n // 2 + 1
        return half + (n % 2) * (8 - 2 * half)

    def over_steps(body):
        def once(n, carry):
            body(step_of(n))
            return carry

        lax.fori_loop(0, 7, once, 0)

    def split_tokens(i, carry):
        lo, hi = to_tiles(tokens[pl.ds(i * 32, 32), :])
        tiles_t[pl.ds(i * 32, 16)] = lo
        tiles_t[pl.ds(i * 32 + 16, 16)] = hi
        return carry

    lax.fori_loop(0, 4, split_tokens, 0)

    def gather(a, h, tiles):
        def once(i, carry):
            for s in range(3):
                stage[a, h, i, s] = tiles[source[(h * 32 + i) * 3 + s]]
            return carry

        lax.fori_loop(0, 32, once, 0, unroll=4)

    gather(0, 0, tiles_t)
    pl.semaphore_wait(barrier, 16)
    over_steps(lambda step: y_copy(0, 0, step).start())
    y_self(0, 0).start()
    gather(0, 1, tiles_t)
    over_steps(lambda step: y_copy(0, 1, step).start())
    y_self(0, 1).start()

    def split_cot(i, carry):
        rows = pl.ds(i * 32, 32)
        cot = (weight[rows, :] * out_grad[rows, :].astype(F32)).astype(BF)
        lo, hi = to_tiles(cot)
        tiles_c[pl.ds(i * 32, 16)] = lo
        tiles_c[pl.ds(i * 32 + 16, 16)] = hi
        return carry

    lax.fori_loop(0, 4, split_cot, 0)
    for h in range(2):
        gather(1, h, tiles_c)
        over_steps(lambda step: y_copy(1, h, step).start())
        y_self(1, h).start()

    def z_copy(a, h, k):
        to = (z + sign * WINDOW[k] + 16) % 16
        return remote(
            mid.at[a, h, to % 4], landed.at[a, h, pl.ds(k * 24, 24)], zs.at[a, h, k], zr.at[a, h, k],
            device(y, to, x, c),
        )

    def z_self(a, h):
        return pltpu.make_async_copy(mid.at[a, h, zl], landed.at[a, h, pl.ds(24, 24)], zl_sem.at[a, h])

    def pass_on(a, h):
        over_steps(lambda step: y_copy(a, h, step).wait_recv())
        y_self(a, h).wait()
        for k in (3, 0, 2):
            z_copy(a, h, k).start()
        z_self(a, h).start()

    def take(a, h, mat):
        for k in (0, 2, 3):
            z_copy(a, h, k).wait_recv()
        z_self(a, h).wait()

        def once(i, carry):
            out = from_tiles(landed[a, h, pl.ds(i * 32, 16)], landed[a, h, pl.ds(i * 32 + 16, 16)])
            lo = pl.multiple_of(h * 96 + i * 32, 32)
            for k in range(16):
                cols = slice(k * LANES, (k + 1) * LANES)
                mat[pl.ds(lo, 16), cols] = out[k * 16 : (k + 1) * 16, :LANES].astype(BF)
                mat[pl.ds(lo + 16, 16), cols] = out[k * 16 : (k + 1) * 16, LANES:].astype(BF)
            return carry

        lax.fori_loop(0, 3, once, 0)

    def rz_copy(a, h, k):
        to = (z - sign * WINDOW[k] + 16) % 16
        return remote(
            ytile.at[a, h, pl.ds(k * 24, 24)], zback.at[a, h, zl], rzs.at[a, h, k], rzr.at[a, h, k],
            device(y, to, x, c),
        )

    def rz_self(a, h):
        return pltpu.make_async_copy(ytile.at[a, h, pl.ds(24, 24)], zback.at[a, h, zl], rzl.at[a, h])

    backs = (back_y, back_r)

    def ry_copy(a, h, step):
        there = (y + step) % 8
        return remote(
            zback.at[a, h, :, pl.ds(there * 3, 3)],
            backs[a].at[pl.ds(h * 32 + y * 4, 4)],
            rys.at[a, h, step - 1],
            ryr.at[a, h, step - 1],
            y_dev(step),
        )

    def ry_self(a, h):
        return pltpu.make_async_copy(
            zback.at[a, h, :, pl.ds(y * 3, 3)], backs[a].at[pl.ds(h * 32 + y * 4, 4)], ryl.at[a, h]
        )

    def send_back(a):
        for h in range(2):
            def once(i, carry):
                lo, hi = to_tiles(mat_y[pl.ds(pl.multiple_of(h * 96 + i * 32, 32), 32), :])
                ytile[a, h, pl.ds(i * 32, 16)] = lo
                ytile[a, h, pl.ds(i * 32 + 16, 16)] = hi
                return carry

            lax.fori_loop(0, 3, once, 0)
            for k in (3, 0, 2):
                rz_copy(a, h, k).start()
            rz_self(a, h).start()

    def pass_back(a, h):
        for k in (0, 2, 3):
            rz_copy(a, h, k).wait_recv()
        rz_self(a, h).wait()
        over_steps(lambda step: ry_copy(a, h, step).start())
        ry_self(a, h).start()

    def contract_back(left, width, weights):
        def once(n, carry):
            at = pl.multiple_of(n * 256, 256)
            out = lax.dot_general(left, weights[pl.ds(at, 256), :], NT, preferred_element_type=F32)
            mat_y[:, pl.ds(at, 256)] = out.astype(BF)
            return carry

        lax.fori_loop(0, D // 256, once, 0)

    for copy in w_copies:
        copy.wait()
    pass_on(0, 0)
    pass_on(0, 1)
    take(0, 0, mat_x)
    take(0, 1, mat_x)

    def gates_once(n, carry):
        at = pl.multiple_of(n * 256, 256)
        gates[:, pl.ds(at, 256)] = jnp.dot(mat_x[...], w1[:, pl.ds(at, 256)], preferred_element_type=F32)
        return carry

    lax.fori_loop(0, F1 // 256, gates_once, 0)

    def hidden_once(n, carry):
        lo = pl.multiple_of(n * LANES, LANES)
        gate = gates[:, pl.ds(lo, LANES)]
        upper = gates[:, pl.ds(lo + F2, LANES)]
        qh[:, pl.ds(lo + F1, LANES)] = (gate * jax.nn.sigmoid(gate) * upper).astype(BF)
        return carry

    lax.fori_loop(0, F2 // LANES, hidden_once, 0)
    contract_back(qh[:, F1:], F2, w2)
    send_back(0)

    pass_on(1, 0)
    pass_on(1, 1)
    pass_back(0, 0)
    pass_back(0, 1)
    take(1, 0, mat_c)
    take(1, 1, mat_c)

    def q_once(n, carry):
        lo = pl.multiple_of(n * LANES, LANES)
        grad = jnp.dot(mat_c[...], w2[:, pl.ds(lo, LANES)], preferred_element_type=F32)
        gate = gates[:, pl.ds(lo, LANES)]
        upper = gates[:, pl.ds(lo + F2, LANES)]
        sig = jax.nn.sigmoid(gate)
        qh[:, pl.ds(lo, LANES)] = (grad * upper * sig * (1.0 + gate * (1.0 - sig))).astype(BF)
        qh[:, pl.ds(lo + F2, LANES)] = (grad * (gate * sig)).astype(BF)
        return carry

    lax.fori_loop(0, F2 // LANES, q_once, 0)

    def turn_once(n, carry):
        lo = pl.multiple_of(n * LANES, LANES)
        same = lax.broadcasted_iota(jnp.int32, (LANES, LANES), 0) == lax.broadcasted_iota(
            jnp.int32, (LANES, LANES), 1
        )
        one = jnp.where(same, 1.0, 0.0).astype(BF)
        qht[pl.ds(lo, LANES), :] = lax.dot_general(
            one, qh[:, pl.ds(lo, LANES)], NT, preferred_element_type=F32
        ).astype(BF)
        return carry

    lax.fori_loop(0, FF // LANES, turn_once, 0)

    def owner(n):
        ahead = jnp.where(n == 0, 2, jnp.where(n == 1, 1, jnp.where(n == 2, 3, 0)))
        return (x + ahead) % 4

    def twin_copy(n, pair):
        at = owner(n)
        return remote(
            part.at[at, pl.ds(pair * 2, 2), pl.ds((1 - c) * FHALF, FHALF)],
            other.at[at, pl.ds(pair * 2, 2)],
            cs.at[n, pair],
            cr.at[n, pair],
            twin,
        )

    def part_once(i, carry):
        n, pair = i // 2, i % 2
        at = owner(n)

        def columns(mat):
            first = pl.multiple_of((pair * 8 + at) * LANES, LANES)
            second = pl.multiple_of((pair * 8 + 4 + at) * LANES, LANES)
            return jnp.concatenate([mat[:, pl.ds(first, LANES)], mat[:, pl.ds(second, LANES)]], axis=1)

        for lo, right in ((0, mat_x), (F2, mat_x), (F1, mat_c)):
            out = jnp.dot(qht[lo : lo + F2, :], columns(right), preferred_element_type=F32).astype(BF)
            part[at, pair * 2, lo : lo + F2] = out[:, :LANES]
            part[at, pair * 2 + 1, lo : lo + F2] = out[:, LANES:]
        twin_copy(n, pair).start()
        return carry

    lax.fori_loop(0, 8, part_once, 0)

    contract_back(qh[:, :F1], F1, w1)
    send_back(1)

    def relay_copy(q, way):
        return remote(
            summed.at[(x + 2) % 4, :, pl.ds(q * FQ + way * FD, FD)],
            xrelay.at[q, way],
            xs.at[q, way],
            xr.at[q, way],
            x_dev(1 - 2 * way),
        )

    def right_copy(q, way):
        src = xacc.at[q, 0] if way == 0 else summed.at[(x + 1) % 4, :, pl.ds(q * FQ + FD, FD)]
        return remote(src, from_l.at[q, :, pl.ds(way * FD, FD)], xs.at[q, 2 + way], xr.at[q, 2 + way], x_dev(1))

    def left_copy(q, way):
        src = xacc.at[q, 1] if way == 1 else summed.at[(x + 3) % 4, :, pl.ds(q * FQ, FD)]
        return remote(src, from_r.at[q, :, pl.ds(way * FD, FD)], xs.at[q, 4 + way], xr.at[q, 4 + way], x_dev(-1))

    def add_twin(n):
        for pair in range(2):
            twin_copy(n, pair).wait_recv()
        at = owner(n)

        def once(k, carry):
            summed[at, k] = part[at, k, pl.ds(pl.multiple_of(c * FHALF, FHALF), FHALF)] + other[at, k]
            return carry

        lax.fori_loop(0, 4, once, 0)

    add_twin(0)
    for q in range(2):
        for way in range(2):
            relay_copy(q, way).start()
    add_twin(1)
    for q in range(2):
        right_copy(q, 1).start()
    add_twin(2)
    for q in range(2):
        left_copy(q, 0).start()
    add_twin(3)
    for q in range(2):
        for way, ahead in ((0, 1), (1, 3)):
            relay_copy(q, way).wait_recv()
            xacc[q, way] = summed[(x + ahead) % 4, :, q * FQ + way * FD : q * FQ + way * FD + FD] + xrelay[q, way]
            (right_copy if way == 0 else left_copy)(q, way).start()

    pass_back(1, 0)
    pass_back(1, 1)

    def zrelay_copy(q, way):
        return remote(
            zsum.at[q, (zh + 2) % 4, pl.ds(way * FD, FD)], zrelay.at[q, way], gs.at[q, way], gr.at[q, way],
            z_dev(4 - 8 * way),
        )

    def up_copy(q, way):
        src = zacc.at[q, 0] if way == 0 else zsum.at[q, (zh + 1) % 4, pl.ds(FD, FD)]
        return remote(src, zfrom_l.at[q, pl.ds(way * FD, FD)], gs.at[q, 2 + way], gr.at[q, 2 + way], z_dev(4))

    def down_copy(q, way):
        src = zacc.at[q, 1] if way == 1 else zsum.at[q, (zh + 3) % 4, pl.ds(0, FD)]
        return remote(src, zfrom_r.at[q, pl.ds(way * FD, FD)], gs.at[q, 4 + way], gr.at[q, 4 + way], z_dev(-4))

    for q in range(2):
        for way in range(2):
            right_copy(q, 1 - way).wait_recv()
            left_copy(q, way).wait_recv()

        def once(k, carry):
            zsum[q, k] = (
                summed[x, k, q * FQ : (q + 1) * FQ].astype(F32)
                + from_l[q, k].astype(F32)
                + from_r[q, k].astype(F32)
            ).astype(BF)
            return carry

        lax.fori_loop(0, 4, once, 0)
        for way in range(2):
            zrelay_copy(q, way).start()
        up_copy(q, 1).start()
        down_copy(q, 0).start()

    def combine(a, scale, out_ref):
        for h in range(2):
            over_steps(lambda step: ry_copy(a, h, step).wait_recv())
            ry_self(a, h).wait()
        back = backs[a]

        def once(i, carry):
            base = i * 32
            first = jnp.stack([back[group[base + t], inner[base + t]] for t in range(16)])
            second = jnp.stack([back[group[base + 16 + t], inner[base + 16 + t]] for t in range(16)])
            out = from_tiles(first, second)
            lo = pl.multiple_of(base, 32)
            for k in range(16):
                cols = slice(k * LANES, (k + 1) * LANES)
                for half in range(2):
                    rows = pl.ds(lo + half * 16, 16)
                    piece = out[k * 16 : (k + 1) * 16, half * LANES : (half + 1) * LANES]
                    if scale:
                        piece = weight[rows, :] * piece
                    out_ref[rows, cols] = piece.astype(BF)
            return carry

        lax.fori_loop(0, 4, once, 0)

    combine(0, True, mixed)

    for q in range(2):
        for way, ahead in ((0, 1), (1, 3)):
            zrelay_copy(q, way).wait_recv()
            zacc[q, way] = zsum[q, (zh + ahead) % 4, way * FD : way * FD + FD] + zrelay[q, way]
            (up_copy if way == 0 else down_copy)(q, way).start()

    def share_copy(q):
        rows = pl.ds(c * FHALF + q * FQ, FQ)
        return remote(final.at[rows], final.at[rows], fs.at[q], fr.at[q], twin)

    for q in range(2):
        for way in range(2):
            up_copy(q, 1 - way).wait_recv()
            down_copy(q, way).wait_recv()
        total = zsum[q, zh].astype(F32) + zfrom_l[q].astype(F32) + zfrom_r[q].astype(F32)
        final[pl.ds(pl.multiple_of(c * FHALF + q * FQ, FQ), FQ)] = (total * (1.0 / 32.0)).astype(BF)
        share_copy(q).start()

    combine(1, False, token_grad)

    for q in range(2):
        share_copy(q).wait_recv()
    pick = (
        lax.broadcasted_iota(jnp.int32, (64, LANES), 1) == lax.broadcasted_iota(jnp.int32, (64, LANES), 0) + c * 64
    )
    pick = jnp.where(pick, 1.0, 0.0).astype(BF)
    grad_in[0] = lax.dot_general(pick, final[:F1], NT, preferred_element_type=F32).astype(BF)
    grad_out[0] = lax.dot_general(pick, final[F1:], NT, preferred_element_type=F32).astype(BF)

    for a in range(2):
        for h in range(2):
            over_steps(lambda step: y_copy(a, h, step).wait_send())
            over_steps(lambda step: ry_copy(a, h, step).wait_send())
            for k in (0, 2, 3):
                z_copy(a, h, k).wait_send()
                rz_copy(a, h, k).wait_send()
    for n in range(4):
        for pair in range(2):
            twin_copy(n, pair).wait_send()
    for q in range(2):
        for way in range(2):
            relay_copy(q, way).wait_send()
            right_copy(q, way).wait_send()
            left_copy(q, way).wait_send()
            zrelay_copy(q, way).wait_send()
            up_copy(q, way).wait_send()
            down_copy(q, way).wait_send()
        share_copy(q).wait_send()


def per_device(tokens, routes, route_weight, w_in, w_out, out_grad):
    source, group, inner = slot_tables(routes)
    smem = pl.BlockSpec(memory_space=pltpu.SMEM)
    vmem = pl.BlockSpec(memory_space=pltpu.VMEM)
    anywhere = pl.BlockSpec(memory_space=pl.ANY)
    dma = pltpu.SemaphoreType.DMA
    tile = (TILE, LANES)
    return pl.pallas_call(
        kernel,
        name="moe",
        out_shape=(
            jax.ShapeDtypeStruct((TOK, D), BF),
            jax.ShapeDtypeStruct((TOK, D), BF),
            jax.ShapeDtypeStruct((1, 64, F1), BF),
            jax.ShapeDtypeStruct((1, 64, F2), BF),
        ),
        in_specs=[smem, smem, smem, vmem, vmem, vmem, anywhere, anywhere],
        out_specs=(vmem, vmem, vmem, vmem),
        scratch_shapes=[
            pltpu.VMEM((D, F1), BF),
            pltpu.VMEM((D, F2), BF),
            pltpu.VMEM((256, 256), BF),
            pltpu.VMEM((TOK + 1, *tile), BF),
            pltpu.VMEM((TOK + 1, *tile), BF),
            pltpu.VMEM((2, 2, 32, 3, *tile), BF),
            pltpu.VMEM((2, 2, 4, 24, *tile), BF),
            pltpu.VMEM((2, 2, 96, *tile), BF),
            pltpu.VMEM((ROWS, D), BF),
            pltpu.VMEM((ROWS, D), BF),
            pltpu.VMEM((ROWS, F1), F32),
            pltpu.VMEM((ROWS, FF), BF),
            pltpu.VMEM((FF, ROWS), BF),
            pltpu.VMEM((ROWS, D), BF),
            pltpu.VMEM((2, 2, 96, *tile), BF),
            pltpu.VMEM((2, 2, 4, 24, *tile), BF),
            pltpu.VMEM((64, 3, *tile), BF),
            pltpu.VMEM((64, 3, *tile), BF),
            pltpu.VMEM((4, 4, FF, LANES), BF),
            pltpu.VMEM((4, 4, FHALF, LANES), BF),
            pltpu.VMEM((4, 4, FHALF, LANES), BF),
            pltpu.VMEM((2, 2, 4, FD, LANES), BF),
            pltpu.VMEM((2, 2, 4, FD, LANES), BF),
            pltpu.VMEM((2, 4, FQ, LANES), BF),
            pltpu.VMEM((2, 4, FQ, LANES), BF),
            pltpu.VMEM((2, 4, FQ, LANES), BF),
            pltpu.VMEM((2, 2, FD, LANES), BF),
            pltpu.VMEM((2, 2, FD, LANES), BF),
            pltpu.VMEM((2, FQ, LANES), BF),
            pltpu.VMEM((2, FQ, LANES), BF),
            pltpu.VMEM((FF, LANES), BF),
            dma((2,)),
            dma((2, 2, 7)), dma((2, 2, 7)), dma((2, 2)),
            dma((2, 2, 4)), dma((2, 2, 4)), dma((2, 2)),
            dma((2, 2, 4)), dma((2, 2, 4)), dma((2, 2)),
            dma((2, 2, 7)), dma((2, 2, 7)), dma((2, 2)),
            dma((4, 2)), dma((4, 2)),
            dma((2, 6)), dma((2, 6)),
            dma((2, 6)), dma((2, 6)),
            dma((2,)), dma((2,)),
        ],
        compiler_params=pltpu.CompilerParams(
            collective_id=0, has_side_effects=True, vmem_limit_bytes=52 << 20
        ),
    )(source, group, inner, tokens, out_grad, route_weight, w_in, w_out)


def solution(mesh):
    rows = P(("expert", "dp"), None)
    whole = P("expert", None, None)
    return jax.shard_map(
        per_device,
        mesh=mesh,
        in_specs=(rows, rows, rows, whole, whole, rows),
        out_specs=(rows, rows, P("expert", "dp", None), P("expert", "dp", None)),
        check_vma=False,
    )
```

```python
import functools

import jax
import jax.numpy as jnp
from jax import lax
from jax.experimental import pallas as pl
from jax.experimental.pallas import tpu as pltpu
from jax.sharding import PartitionSpec as P

MESH = pl.DeviceIdType.MESH
BF = jnp.bfloat16
F32 = jnp.float32

D = 2048
F1 = 768
F2 = 384
FF = F1 + F2
ROWS = 192
TOK = 128
LANES = 128
TILE = 16
NH = 3
SP = 6 // NH
PART = ROWS // NH
FHALF = FF // 2
NQ = 6
FQ = FHALF // NQ
FD = FQ // 2
NT = (((1,), (1,)), ((), ()))
WINDOW = (-1, 0, 1, 2)


def kernel(
    routes, weights, tokens_any, grad_any, w1_any, w2_any,
    mixed, token_grad, grad_in, grad_out,
    tokens, out_grad, weight, table, slots, w1, w2, perm, tiles_t, tiles_c, stage, mid, landed, mat_x, mat_c, gates, qh, qht, mat_y,
    ytile, zback, back_y, back_r, part, other, summed,
    xrelay, xacc, from_l, from_r, zsum, zrelay, zacc, zfrom_l, zfrom_r, final,
    io_sem, w_sem, ys, yr, yl, zs, zr, zl_sem, rzs, rzr, rzl, rys, ryr, ryl,
    cs, cr, xs, xr, gs, gr, fs, fr,
):
    e = lax.axis_index("expert")
    d = lax.axis_index("dp")
    y, zl = e // 4, e % 4
    zh, x, c = d // 8, (d // 2) % 4, d % 2
    z = zh * 4 + zl
    sign = 1 - 2 * c

    def device(y_at, z_at, x_at, c_at):
        return {"expert": y_at * 4 + z_at % 4, "dp": (z_at // 4) * 8 + x_at * 2 + c_at}

    def y_dev(step):
        return device((y + step) % 8, z, x, c)

    def z_dev(step):
        return device(y, (z + step + 16) % 16, x, c)

    def x_dev(step):
        return device(y, z, (x + step + 4) % 4, c)

    twin = device(y, z, x, 1 - c)

    def remote(src, dst, send, recv, to):
        return pltpu.make_async_remote_copy(
            src_ref=src, dst_ref=dst, send_sem=send, recv_sem=recv, device_id=to, device_id_type=MESH
        )

    io_copies = (
        pltpu.make_async_copy(tokens_any, tokens, io_sem.at[0]),
        pltpu.make_async_copy(grad_any, out_grad, io_sem.at[1]),
    )
    w_copies = (
        pltpu.make_async_copy(w1_any.at[0], w1, w_sem.at[0]),
        pltpu.make_async_copy(w2_any.at[0], w2, w_sem.at[1]),
    )
    for copy in io_copies:
        copy.start()
    barrier = pltpu.get_barrier_semaphore()

    def greet(to):
        pl.semaphore_signal(barrier, inc=1, device_id=to, device_id_type=MESH)

    for step in range(1, 8):
        greet(y_dev(step))
    for step in (-4, -2, -1, 1, 2, 4):
        greet(z_dev(step))
    for step in (-1, 1):
        greet(x_dev(step))
    greet(twin)

    for copy in w_copies:
        copy.start()

    chosen = routes[...]
    by_col = jnp.broadcast_to(chosen.astype(F32), (TOK, TOK))
    earlier = lax.broadcasted_iota(jnp.int32, (TOK, TOK), 0) < lax.broadcasted_iota(jnp.int32, (TOK, TOK), 1)
    same = (by_col == jnp.transpose(by_col)) & earlier
    rank = jnp.sum(jnp.where(same, 1, 0), axis=0, keepdims=True)
    group_of = (rank // SP) * 32 + chosen
    inner_of = rank % SP
    place = jnp.broadcast_to((group_of * SP + inner_of).astype(F32), (2 * TOK, TOK))
    slot_at = lax.broadcasted_iota(jnp.int32, (TOK, 2 * TOK), 1).astype(F32)
    token_at = lax.broadcasted_iota(jnp.int32, (TOK, 2 * TOK), 0)
    holds = jnp.transpose(place) == slot_at
    table[...] = jnp.zeros_like(table)
    token_of = TOK + jnp.sum(jnp.where(holds, token_at - TOK, 0), axis=0, keepdims=True)
    table[0:1, :] = jnp.clip(token_of, 0, TOK)
    table[1:2, :TOK] = jnp.clip(group_of, 0, NH * 32 - 1)
    table[2:3, :TOK] = inner_of
    table_copy = pltpu.make_async_copy(table, slots, io_sem.at[2])
    table_copy.start()
    weight[...] = jnp.transpose(jnp.broadcast_to(weights[...], (TOK, TOK)))

    row_at = lax.broadcasted_iota(jnp.int32, (256, 256), 0)
    col_at = lax.broadcasted_iota(jnp.int32, (256, 256), 1)
    perm[...] = jnp.where(col_at == (row_at % 16) * 16 + row_at // 16, 1.0, 0.0).astype(BF)

    def to_tiles(rows32):
        cols = [
            jnp.concatenate(
                [rows32[:16, k * LANES : (k + 1) * LANES], rows32[16:, k * LANES : (k + 1) * LANES]], axis=1
            )
            for k in range(16)
        ]
        out = jnp.dot(perm[...], jnp.concatenate(cols, axis=0), preferred_element_type=F32).astype(BF)
        return out[:, :LANES].reshape(16, TILE, LANES), out[:, LANES:].reshape(16, TILE, LANES)

    def from_tiles(first, second):
        both = jnp.concatenate([first.reshape(256, LANES), second.reshape(256, LANES)], axis=1)
        return jnp.dot(perm[...], both, preferred_element_type=F32)

    tiles_t[TOK] = jnp.zeros((TILE, LANES), BF)
    tiles_c[TOK] = jnp.zeros((TILE, LANES), BF)

    def y_copy(a, h, step):
        there = (y + step) % 8
        return remote(
            stage.at[a, h, pl.ds(there * 4, 4)],
            mid.at[a, h, :, pl.ds(y * SP, SP)],
            ys.at[a, h, step - 1],
            yr.at[a, h, step - 1],
            y_dev(step),
        )

    def y_self(a, h):
        return pltpu.make_async_copy(
            stage.at[a, h, pl.ds(y * 4, 4)], mid.at[a, h, :, pl.ds(y * SP, SP)], yl.at[a, h]
        )

    def step_of(n):
        half = n // 2 + 1
        return half + (n % 2) * (8 - 2 * half)

    def over_steps(body):
        def once(n, carry):
            body(step_of(n))
            return carry

        lax.fori_loop(0, 7, once, 0)

    def split_tokens(i, carry):
        lo, hi = to_tiles(tokens[pl.ds(i * 32, 32), :])
        tiles_t[pl.ds(i * 32, 16)] = lo
        tiles_t[pl.ds(i * 32 + 16, 16)] = hi
        return carry

    io_copies[0].wait()
    lax.fori_loop(0, 4, split_tokens, 0, unroll=2)

    def gather(a, h, tiles):
        def once(i, carry):
            for s in range(SP):
                stage[a, h, i, s] = tiles[slots[0, (h * 32 + i) * SP + s]]
            return carry

        lax.fori_loop(0, 32, once, 0, unroll=4)

    def y_start(a, h):
        over_steps(lambda step: y_copy(a, h, step).start())
        y_self(a, h).start()

    table_copy.wait()
    gather(0, 0, tiles_t)
    pl.semaphore_wait(barrier, 16)
    y_start(0, 0)
    for h in range(1, NH):
        gather(0, h, tiles_t)
        y_start(0, h)

    def split_cot(i, carry):
        rows = pl.ds(i * 32, 32)
        scale = jnp.concatenate([weight[rows, :]] * 16, axis=1)
        cot = (scale * out_grad[rows, :].astype(F32)).astype(BF)
        lo, hi = to_tiles(cot)
        tiles_c[pl.ds(i * 32, 16)] = lo
        tiles_c[pl.ds(i * 32 + 16, 16)] = hi
        return carry

    io_copies[1].wait()
    lax.fori_loop(0, 4, split_cot, 0, unroll=2)
    for h in range(NH):
        gather(1, h, tiles_c)

    def z_copy(a, h, k):
        to = (z + sign * WINDOW[k] + 16) % 16
        return remote(
            mid.at[a, h, to % 4], landed.at[a, h, pl.ds(k * 8 * SP, 8 * SP)], zs.at[a, h, k], zr.at[a, h, k],
            device(y, to, x, c),
        )

    def z_self(a, h):
        return pltpu.make_async_copy(mid.at[a, h, zl], landed.at[a, h, pl.ds(8 * SP, 8 * SP)], zl_sem.at[a, h])

    def pass_on(a, h):
        over_steps(lambda step: y_copy(a, h, step).wait_recv())
        y_self(a, h).wait()
        for k in (3, 0, 2):
            z_copy(a, h, k).start()
        z_self(a, h).start()

    def take(a, h, mat):
        for k in (0, 2, 3):
            z_copy(a, h, k).wait_recv()
        z_self(a, h).wait()

        def once(i, carry):
            out = from_tiles(landed[a, h, pl.ds(i * 32, 16)], landed[a, h, pl.ds(i * 32 + 16, 16)])
            lo = pl.multiple_of(h * PART + i * 32, 32)
            for k in range(16):
                cols = slice(k * LANES, (k + 1) * LANES)
                mat[pl.ds(lo, 16), cols] = out[k * 16 : (k + 1) * 16, :LANES].astype(BF)
                mat[pl.ds(lo + 16, 16), cols] = out[k * 16 : (k + 1) * 16, LANES:].astype(BF)
            return carry

        lax.fori_loop(0, PART // 32, once, 0, unroll=True)

    def rz_copy(a, h, k):
        to = (z - sign * WINDOW[k] + 16) % 16
        return remote(
            ytile.at[a, h, pl.ds(k * 8 * SP, 8 * SP)], zback.at[a, h, zl], rzs.at[a, h, k], rzr.at[a, h, k],
            device(y, to, x, c),
        )

    def rz_self(a, h):
        return pltpu.make_async_copy(ytile.at[a, h, pl.ds(8 * SP, 8 * SP)], zback.at[a, h, zl], rzl.at[a, h])

    backs = (back_y, back_r)

    def ry_copy(a, h, step):
        there = (y + step) % 8
        return remote(
            zback.at[a, h, :, pl.ds(there * SP, SP)],
            backs[a].at[pl.ds(h * 32 + y * 4, 4)],
            rys.at[a, h, step - 1],
            ryr.at[a, h, step - 1],
            y_dev(step),
        )

    def ry_self(a, h):
        return pltpu.make_async_copy(
            zback.at[a, h, :, pl.ds(y * SP, SP)], backs[a].at[pl.ds(h * 32 + y * 4, 4)], ryl.at[a, h]
        )

    def z_back(a, h):
        for k in (3, 0, 2):
            rz_copy(a, h, k).start()
        rz_self(a, h).start()

    def send_back(a, now):
        for h in range(NH):
            def once(i, carry):
                lo, hi = to_tiles(mat_y[pl.ds(pl.multiple_of(h * PART + i * 32, 32), 32), :])
                ytile[a, h, pl.ds(i * 32, 16)] = lo
                ytile[a, h, pl.ds(i * 32 + 16, 16)] = hi
                return carry

            lax.fori_loop(0, PART // 32, once, 0, unroll=True)
            if h < now:
                z_back(a, h)

    def pass_back(a, h):
        for k in (0, 2, 3):
            rz_copy(a, h, k).wait_recv()
        rz_self(a, h).wait()
        over_steps(lambda step: ry_copy(a, h, step).start())
        ry_self(a, h).start()

    def contract_back(left, width, weights):
        def once(n, carry):
            at = pl.multiple_of(n * 256, 256)
            out = lax.dot_general(left, weights[pl.ds(at, 256), :], NT, preferred_element_type=F32)
            mat_y[:, pl.ds(at, 256)] = out.astype(BF)
            return carry

        lax.fori_loop(0, D // 256, once, 0, unroll=2)

    for copy in w_copies:
        copy.wait()
    for h in range(NH):
        pass_on(0, h)
        y_start(1, h)
    for h in range(NH):
        take(0, h, mat_x)

    def gates_once(n, carry):
        at = pl.multiple_of(n * 256, 256)
        gates[:, pl.ds(at, 256)] = jnp.dot(mat_x[...], w1[:, pl.ds(at, 256)], preferred_element_type=F32)
        return carry

    lax.fori_loop(0, F1 // 256, gates_once, 0, unroll=True)

    def hidden_once(n, carry):
        lo = pl.multiple_of(n * LANES, LANES)
        gate = gates[:, pl.ds(lo, LANES)]
        upper = gates[:, pl.ds(lo + F2, LANES)]
        qh[:, pl.ds(lo + F1, LANES)] = (gate * jax.nn.sigmoid(gate) * upper).astype(BF)
        return carry

    lax.fori_loop(0, F2 // LANES, hidden_once, 0, unroll=True)
    pass_on(1, 0)
    contract_back(qh[:, F1:], F2, w2)
    send_back(0, 1)

    for h in range(1, NH):
        pass_on(1, h)
    pass_back(0, 0)
    for h in range(NH):
        take(1, h, mat_c)
        if h >= 1:
            z_back(0, h)

    def q_once(n, carry):
        lo = pl.multiple_of(n * LANES, LANES)
        grad = jnp.dot(mat_c[...], w2[:, pl.ds(lo, LANES)], preferred_element_type=F32)
        gate = gates[:, pl.ds(lo, LANES)]
        upper = gates[:, pl.ds(lo + F2, LANES)]
        sig = jax.nn.sigmoid(gate)
        qh[:, pl.ds(lo, LANES)] = (grad * upper * sig * (1.0 + gate * (1.0 - sig))).astype(BF)
        qh[:, pl.ds(lo + F2, LANES)] = (grad * (gate * sig)).astype(BF)
        return carry

    lax.fori_loop(0, F2 // LANES, q_once, 0, unroll=True)

    def turn_once(n, carry):
        lo = pl.multiple_of(n * LANES, LANES)
        same = lax.broadcasted_iota(jnp.int32, (LANES, LANES), 0) == lax.broadcasted_iota(
            jnp.int32, (LANES, LANES), 1
        )
        one = jnp.where(same, 1.0, 0.0).astype(BF)
        qht[pl.ds(lo, LANES), :] = lax.dot_general(
            one, qh[:, pl.ds(lo, LANES)], NT, preferred_element_type=F32
        ).astype(BF)
        return carry

    lax.fori_loop(0, FF // LANES, turn_once, 0, unroll=3)

    def owner(n):
        return (x + (2, 1, 3, 0)[n]) % 4

    def twin_copy(n, pair):
        at = owner(n)
        return remote(
            part.at[at, pl.ds(pair * 2, 2), pl.ds((1 - c) * FHALF, FHALF)],
            other.at[at, pl.ds(pair * 2, 2)],
            cs.at[n, pair],
            cr.at[n, pair],
            twin,
        )

    def part_once(n, pair):
        at = owner(n)

        def columns(mat):
            first = pl.multiple_of((pair * 8 + at) * LANES, LANES)
            second = pl.multiple_of((pair * 8 + 4 + at) * LANES, LANES)
            return jnp.concatenate([mat[:, pl.ds(first, LANES)], mat[:, pl.ds(second, LANES)]], axis=1)

        for lo, right in ((0, mat_x), (F2, mat_x), (F1, mat_c)):
            out = jnp.dot(qht[lo : lo + F2, :], columns(right), preferred_element_type=F32).astype(BF)
            part[at, pair * 2, lo : lo + F2] = out[:, :LANES]
            part[at, pair * 2 + 1, lo : lo + F2] = out[:, LANES:]
        twin_copy(n, pair).start()

    def relay_copy(q, way):
        return remote(
            summed.at[(x + 2) % 4, :, pl.ds(q * FQ + way * FD, FD)],
            xrelay.at[q, way],
            xs.at[q, way],
            xr.at[q, way],
            x_dev(1 - 2 * way),
        )

    def right_copy(q, way):
        src = xacc.at[q, 0] if way == 0 else summed.at[(x + 1) % 4, :, pl.ds(q * FQ + FD, FD)]
        return remote(src, from_l.at[q, :, pl.ds(way * FD, FD)], xs.at[q, 2 + way], xr.at[q, 2 + way], x_dev(1))

    def left_copy(q, way):
        src = xacc.at[q, 1] if way == 1 else summed.at[(x + 3) % 4, :, pl.ds(q * FQ, FD)]
        return remote(src, from_r.at[q, :, pl.ds(way * FD, FD)], xs.at[q, 4 + way], xr.at[q, 4 + way], x_dev(-1))

    def add_twin(n):
        for pair in range(2):
            twin_copy(n, pair).wait_recv()
        at = owner(n)

        def once(k, carry):
            summed[at, k] = part[at, k, pl.ds(pl.multiple_of(c * FHALF, FHALF), FHALF)] + other[at, k]
            return carry

        lax.fori_loop(0, 4, once, 0)

    def zrelay_copy(q, way):
        return remote(
            zsum.at[q, (zh + 2) % 4, pl.ds(way * FD, FD)], zrelay.at[q, way], gs.at[q, way], gr.at[q, way],
            z_dev(4 - 8 * way),
        )

    def up_copy(q, way):
        src = zacc.at[q, 0] if way == 0 else zsum.at[q, (zh + 1) % 4, pl.ds(FD, FD)]
        return remote(src, zfrom_l.at[q, pl.ds(way * FD, FD)], gs.at[q, 2 + way], gr.at[q, 2 + way], z_dev(4))

    def down_copy(q, way):
        src = zacc.at[q, 1] if way == 1 else zsum.at[q, (zh + 3) % 4, pl.ds(0, FD)]
        return remote(src, zfrom_r.at[q, pl.ds(way * FD, FD)], gs.at[q, 4 + way], gr.at[q, 4 + way], z_dev(-4))

    def combine(a, scale, out_ref):
        for h in range(NH):
            over_steps(lambda step: ry_copy(a, h, step).wait_recv())
            ry_self(a, h).wait()
        back = backs[a]

        def once(i, carry):
            base = i * 32
            first = jnp.stack([back[slots[1, base + t], slots[2, base + t]] for t in range(16)])
            second = jnp.stack([back[slots[1, base + 16 + t], slots[2, base + 16 + t]] for t in range(16)])
            out = from_tiles(first, second)
            lo = pl.multiple_of(base, 32)
            for k in range(16):
                cols = slice(k * LANES, (k + 1) * LANES)
                for half in range(2):
                    rows = pl.ds(lo + half * 16, 16)
                    piece = out[k * 16 : (k + 1) * 16, half * LANES : (half + 1) * LANES]
                    if scale:
                        piece = weight[rows, :] * piece
                    out_ref[rows, cols] = piece.astype(BF)
            return carry

        lax.fori_loop(0, 4, once, 0)

    def share_copy(q):
        rows = pl.ds(c * FHALF + q * FQ, FQ)
        return remote(final.at[rows], final.at[rows], fs.at[q], fr.at[q], twin)

    def x_relay(q):
        for way in range(2):
            relay_copy(q, way).start()

    def x_start(q):
        right_copy(q, 1).start()
        left_copy(q, 0).start()

    def x_forward(q):
        for way, ahead in ((0, 1), (1, 3)):
            relay_copy(q, way).wait_recv()
            lo = q * FQ + way * FD
            xacc[q, way] = summed[(x + ahead) % 4, :, lo : lo + FD] + xrelay[q, way]
            (right_copy if way == 0 else left_copy)(q, way).start()

    def z_start(q):
        for way in range(2):
            right_copy(q, 1 - way).wait_recv()
            left_copy(q, way).wait_recv()
        zsum[q] = (
            summed[x, :, q * FQ : (q + 1) * FQ].astype(F32) + from_l[q].astype(F32) + from_r[q].astype(F32)
        ).astype(BF)
        for way in range(2):
            zrelay_copy(q, way).start()
        up_copy(q, 1).start()
        down_copy(q, 0).start()

    def z_forward(q):
        for way, ahead in ((0, 1), (1, 3)):
            zrelay_copy(q, way).wait_recv()
            zacc[q, way] = zsum[q, (zh + ahead) % 4, way * FD : way * FD + FD] + zrelay[q, way]
            (up_copy if way == 0 else down_copy)(q, way).start()

    def share_start(q):
        for way in range(2):
            up_copy(q, 1 - way).wait_recv()
            down_copy(q, way).wait_recv()
        total = zsum[q, zh].astype(F32) + zfrom_l[q].astype(F32) + zfrom_r[q].astype(F32)
        final[pl.ds(pl.multiple_of(c * FHALF + q * FQ, 32), FQ)] = (total * (1.0 / 32.0)).astype(BF)
        share_copy(q).start()

    for n in range(4):
        for pair in range(2):
            part_once(n, pair)
    pass_back(0, 1)
    add_twin(0)
    for q in range(3):
        x_relay(q)
    add_twin(1)
    for q in range(2):
        right_copy(q, 1).start()
    add_twin(2)
    for q in range(2):
        left_copy(q, 0).start()
    add_twin(3)
    contract_back(qh[:, :F1], F1, w1)
    send_back(1, NH)
    pass_back(0, 2)

    for s in range(NQ + 8):
        if s < NQ:
            x_forward(s)
        if s + 3 < NQ:
            x_relay(s + 3)
        if s + 2 < NQ:
            x_start(s + 2)
        if 2 <= s <= NQ + 1:
            z_start(s - 2)
        if 2 <= s < NH + 2:
            pass_back(1, s - 2)
        if 5 <= s <= NQ + 4:
            z_forward(s - 5)
        if 8 <= s:
            share_start(s - 8)
        if s == NQ + 2:
            combine(0, True, mixed)

    combine(1, False, token_grad)

    for q in range(NQ):
        share_copy(q).wait_recv()
    pick = (
        lax.broadcasted_iota(jnp.int32, (64, LANES), 1) == lax.broadcasted_iota(jnp.int32, (64, LANES), 0) + c * 64
    )
    pick = jnp.where(pick, 1.0, 0.0).astype(BF)
    grad_in[0] = lax.dot_general(pick, final[:F1], NT, preferred_element_type=F32).astype(BF)
    grad_out[0] = lax.dot_general(pick, final[F1:], NT, preferred_element_type=F32).astype(BF)

    for a in range(2):
        for h in range(NH):
            over_steps(lambda step: y_copy(a, h, step).wait_send())
            over_steps(lambda step: ry_copy(a, h, step).wait_send())
            for k in (0, 2, 3):
                z_copy(a, h, k).wait_send()
                rz_copy(a, h, k).wait_send()
    for n in range(4):
        for pair in range(2):
            twin_copy(n, pair).wait_send()
    for q in range(NQ):
        for way in range(2):
            relay_copy(q, way).wait_send()
            right_copy(q, way).wait_send()
            left_copy(q, way).wait_send()
            zrelay_copy(q, way).wait_send()
            up_copy(q, way).wait_send()
            down_copy(q, way).wait_send()
        share_copy(q).wait_send()


def per_device(tokens, routes, route_weight, w_in, w_out, out_grad):
    vmem = pl.BlockSpec(memory_space=pltpu.VMEM)
    anywhere = pl.BlockSpec(memory_space=pltpu.HBM)
    dma = pltpu.SemaphoreType.DMA
    tile = (TILE, LANES)
    shapes = (
        jax.ShapeDtypeStruct((TOK, D), BF),
        jax.ShapeDtypeStruct((TOK, D), BF),
        jax.ShapeDtypeStruct((1, 64, F1), BF),
        jax.ShapeDtypeStruct((1, 64, F2), BF),
    )
    return pl.pallas_call(
        kernel,
        name="moe",
        out_shape=shapes,
        in_specs=[vmem, vmem, anywhere, anywhere, anywhere, anywhere],
        out_specs=(vmem, vmem, vmem, vmem),
        scratch_shapes=[
            pltpu.VMEM((TOK, D), BF),
            pltpu.VMEM((TOK, D), BF),
            pltpu.VMEM((TOK, TOK), F32),
            pltpu.VMEM((8, 2 * TOK), jnp.int32),
            pltpu.SMEM((8, 2 * TOK), jnp.int32),
            pltpu.VMEM((D, F1), BF),
            pltpu.VMEM((D, F2), BF),
            pltpu.VMEM((256, 256), BF),
            pltpu.VMEM((TOK + 1, *tile), BF),
            pltpu.VMEM((TOK + 1, *tile), BF),
            pltpu.VMEM((2, NH, 32, SP, *tile), BF),
            pltpu.VMEM((2, NH, 4, 8 * SP, *tile), BF),
            pltpu.VMEM((2, NH, PART, *tile), BF),
            pltpu.VMEM((ROWS, D), BF),
            pltpu.VMEM((ROWS, D), BF),
            pltpu.VMEM((ROWS, F1), F32),
            pltpu.VMEM((ROWS, FF), BF),
            pltpu.VMEM((FF, ROWS), BF),
            pltpu.VMEM((ROWS, D), BF),
            pltpu.VMEM((2, NH, PART, *tile), BF),
            pltpu.VMEM((2, NH, 4, 8 * SP, *tile), BF),
            pltpu.VMEM((NH * 32, SP, *tile), BF),
            pltpu.VMEM((NH * 32, SP, *tile), BF),
            pltpu.VMEM((4, 4, FF, LANES), BF),
            pltpu.VMEM((4, 4, FHALF, LANES), BF),
            pltpu.VMEM((4, 4, FHALF, LANES), BF),
            pltpu.VMEM((NQ, 2, 4, FD, LANES), BF),
            pltpu.VMEM((NQ, 2, 4, FD, LANES), BF),
            pltpu.VMEM((NQ, 4, FQ, LANES), BF),
            pltpu.VMEM((NQ, 4, FQ, LANES), BF),
            pltpu.VMEM((NQ, 4, FQ, LANES), BF),
            pltpu.VMEM((NQ, 2, FD, LANES), BF),
            pltpu.VMEM((NQ, 2, FD, LANES), BF),
            pltpu.VMEM((NQ, FQ, LANES), BF),
            pltpu.VMEM((NQ, FQ, LANES), BF),
            pltpu.VMEM((FF, LANES), BF),
            dma((3,)),
            dma((2,)),
            dma((2, NH, 7)), dma((2, NH, 7)), dma((2, NH)),
            dma((2, NH, 4)), dma((2, NH, 4)), dma((2, NH)),
            dma((2, NH, 4)), dma((2, NH, 4)), dma((2, NH)),
            dma((2, NH, 7)), dma((2, NH, 7)), dma((2, NH)),
            dma((4, 2)), dma((4, 2)),
            dma((NQ, 6)), dma((NQ, 6)),
            dma((NQ, 6)), dma((NQ, 6)),
            dma((NQ,)), dma((NQ,)),
        ],
        compiler_params=pltpu.CompilerParams(
            collective_id=0, has_side_effects=True, vmem_limit_bytes=52 << 20
        ),
    )(routes.reshape(1, TOK), route_weight.reshape(1, TOK), tokens, out_grad, w_in, w_out)


def solution(mesh):
    rows = P(("expert", "dp"), None)
    whole = P("expert", None, None)
    return jax.shard_map(
        per_device,
        mesh=mesh,
        in_specs=(rows, rows, rows, whole, whole, rows),
        out_specs=(rows, rows, P("expert", "dp", None), P("expert", "dp", None)),
        check_vma=False,
    )
```
